32 devices in a mesh: groups: 2 (over y), wide: 4 (over z), narrow: 4 (over x, core).
Axes of the slice: x: 2, y: 2, z: 4, core: 2. Of those that a mesh axis runs over, the one named last changes fastest.
Arguments:
- hidden: bfloat16 [96, 8192], P(('groups', 'wide')), parts along dimension 0, may hold values from -6 to 6
- attention_norm_gain: bfloat16 [8192], replicated, may hold values from 0.5 to 1.5
- row_adapter_index: int32 [96], P(('groups', 'wide')), parts along dimension 0, may hold values from 0 to 31
- lengths: int32 [96], P(('groups', 'wide')), parts along dimension 0, may hold values from 1 to 192, as said below
- paged_key_cache: bfloat16 [96, 8, 192, 128], P(('groups', 'wide'), 'narrow'), parts along dimension 0, may hold values from -510 to 510
- paged_value_cache: bfloat16 [96, 8, 192, 128], P(('groups', 'wide'), 'narrow'), parts along dimension 0, may hold values from -6 to 6
- query_weight: bfloat16 [8192, 8192], P('wide', 'narrow'), may hold values from -0.0625 to 0.0625
- key_weight: bfloat16 [8192, 1024], P('wide', 'narrow'), may hold values from -0.0625 to 0.0625
- value_weight: bfloat16 [8192, 1024], P('wide', 'narrow'), may hold values from -0.0625 to 0.0625
- adapter_down_weight: bfloat16 [64, 3, 64, 8192], P(('groups', 'wide'), None, None, 'narrow'), parts along dimension 0, may hold values from -0.0625 to 0.0625
- adapter_up_query: bfloat16 [64, 64, 8192], P(('groups', 'wide'), None, 'narrow'), parts along dimension 0, may hold values from -0.75 to 0.75
- adapter_up_key_value: bfloat16 [64, 2, 64, 1024], P(('groups', 'wide'), None, None, 'narrow'), parts along dimension 0, may hold values from -0.75 to 0.75
Outputs:
- attention: bfloat16 [96, 8192], P(('groups', 'wide'), 'narrow'), parts along dimension 0
The draws below stay inside these ranges and needn't reach their ends.
There are 2 independent parts, one for each index of `groups`. The reference program is written for one: setup_inputs(seed, part) draws one part's arguments, and reference() takes and returns one part's arrays. A program takes and returns all parts, laid end to end along the dimension named above; an argument that names none is the same for every part. Nothing has to cross between parts.
Inputs may be any that keep to these rules, and one draw needn't show every extreme that they name: Row r's cache holds keys and values at positions 0 to lengths[r] - 1; some row has all 192.
All inputs are finite; a program needn't handle non-finite values.
Results may differ from the reference program's by a relative error of at most 0.008.
The reference program's roundings to bfloat16 on the way count: a program that leaves them out, or rounds other values in their place, can miss the bound.
Values may be sent and summed in bfloat16 or wider, within the bound.
No kernel may reach another device: no remote copies, remote signals or barrier semaphores. Data moves between devices by JAX's collectives and lax.ppermute only.
A program may use at most 64 MiB of HBM per device.

```python
import math
import jax
import jax.numpy as jnp
import numpy as np
from jax import lax

MODEL_WIDTH = 8192
QUERY_HEADS = 64
KEY_VALUE_HEADS = 8
HEAD_WIDTH = 128
ADAPTER_RANK = 64
CACHE = 192
ADAPTER_COUNT = 32
ROWS = 48


def draw_lengths(key, part):
    key = jax.random.fold_in(key, 11)
    first_key, second_key, third_key = jax.random.split(key, 3)
    uniform_part = jax.random.randint(first_key, (ROWS,), 0, CACHE)
    skew_part = jax.random.randint(second_key, (ROWS,), 0, CACHE)
    drawn = 1 + uniform_part * skew_part // CACHE
    chosen = jax.random.randint(third_key, (), 0, ROWS)
    return jnp.where(jnp.arange(ROWS) == chosen, CACHE, drawn).astype(jnp.int32)


def draw_paged_key_cache(key, part):
    key = jax.random.fold_in(key, 23)
    value_key = jax.random.fold_in(key, 0)
    cache_shape = (ROWS, KEY_VALUE_HEADS, CACHE, HEAD_WIDTH)
    return jnp.clip(jax.random.normal(value_key, cache_shape, jnp.float32), -6.0, 6.0).astype(jnp.bfloat16)


def place_ends(result, rng, low, largest):
    spot = [jax.random.randint(jax.random.fold_in(rng, axis), (), 0, length) for axis, length in enumerate(result.shape)]
    main_axis = result.shape.index(max(result.shape))
    neighbour = spot[:main_axis] + [(spot[main_axis] + 1) % result.shape[main_axis]] + spot[main_axis + 1:]
    return result.at[tuple(spot)].set(low).at[tuple(neighbour)].set(largest)


def steps_of(own_key, extent, cuts, low, largest):
    gain = 1.0
    for dim, blocks in cuts:
        steps = jax.random.uniform(jax.random.fold_in(jax.random.fold_in(own_key, 6), dim), (blocks,), jnp.float32, low / len(cuts), largest / len(cuts))
        gain = gain * jnp.repeat(jnp.exp(steps), extent[dim] // blocks).reshape((-1,) + (1,) * (len(extent) - 1 - dim))
    return gain


def rank_table(amount, slope):
    weights = [(1 << 20) // math.isqrt(standing ** slope) + 1 for standing in range(1, amount + 1)]
    width = 1 + sum(weights) // (1 << 30)
    return np.cumsum(np.array([max(1, weight // width) for weight in weights]))


def ranked_ids(rng, shape, amount, lean):
    grid = rank_table(amount, lean)
    pick = jax.random.randint(jax.random.fold_in(rng, 1), shape, 0, int(grid[amount - 1]))
    rank = jnp.searchsorted(jnp.asarray(grid, jnp.int32), pick, side="right")
    return jax.random.permutation(jax.random.fold_in(rng, 2), amount)[rank].astype(jnp.int32)


def normal_values(key, dims, spread, most, cuts=(), held_as=jnp.bfloat16):
    entries = spread * jax.random.normal(key, dims, jnp.float32)
    if cuts:
        entries = entries * steps_of(key, dims, cuts, -0.22, 0.18)
    return jnp.clip(entries, -most, most).astype(held_as)


def setup_inputs(seed: int = 0, part: int = 0) -> dict:
    key_of = jax.random.split(jax.random.key(seed), 13)
    part_keys = jax.random.split(jax.random.fold_in(key_of[12], part), 13)
    hidden = normal_values(part_keys[0], (ROWS, MODEL_WIDTH), 1.0, 6.0, ((0, 4),))
    attention_norm_gain = jnp.clip(1.0 + 0.1 * jax.random.normal(key_of[1], (MODEL_WIDTH,), jnp.float32), 0.5, 1.5).astype(jnp.bfloat16)
    row_adapter_index = place_ends(ranked_ids(part_keys[2], (ROWS,), ADAPTER_COUNT, 2), jax.random.fold_in(part_keys[2], 3), 0, ADAPTER_COUNT - 1).astype(jnp.int32)
    lengths = draw_lengths(jax.random.fold_in(jax.random.fold_in(key_of[12], part), 71), part)
    paged_key_cache = draw_paged_key_cache(jax.random.fold_in(jax.random.fold_in(key_of[12], part), 71), part)
    paged_value_cache = normal_values(part_keys[5], (ROWS, KEY_VALUE_HEADS, CACHE, HEAD_WIDTH), 1.0, 6.0, ((0, 4), (1, 4)))
    query_weight = normal_values(key_of[6], (MODEL_WIDTH, QUERY_HEADS * HEAD_WIDTH), MODEL_WIDTH ** -0.5, 0.0625, ((0, 4), (1, 4)))
    key_weight = normal_values(key_of[7], (MODEL_WIDTH, KEY_VALUE_HEADS * HEAD_WIDTH), MODEL_WIDTH ** -0.5, 0.0625, ((0, 4), (1, 4)))
    value_weight = normal_values(key_of[8], (MODEL_WIDTH, KEY_VALUE_HEADS * HEAD_WIDTH), MODEL_WIDTH ** -0.5, 0.0625, ((0, 4), (1, 4)))
    adapter_down_weight = normal_values(part_keys[9], (ADAPTER_COUNT, 3, ADAPTER_RANK, MODEL_WIDTH), MODEL_WIDTH ** -0.5, 0.0625, ((0, 4), (3, 4)))
    adapter_up_query = normal_values(part_keys[10], (ADAPTER_COUNT, ADAPTER_RANK, QUERY_HEADS * HEAD_WIDTH), ADAPTER_RANK ** -0.5, 0.75, ((0, 4), (2, 4)))
    adapter_up_key_value = normal_values(part_keys[11], (ADAPTER_COUNT, 2, ADAPTER_RANK, KEY_VALUE_HEADS * HEAD_WIDTH), ADAPTER_RANK ** -0.5, 0.75, ((0, 4), (3, 4)))
    return dict(hidden=hidden, attention_norm_gain=attention_norm_gain, row_adapter_index=row_adapter_index, lengths=lengths, paged_key_cache=paged_key_cache, paged_value_cache=paged_value_cache, query_weight=query_weight, key_weight=key_weight, value_weight=value_weight, adapter_down_weight=adapter_down_weight, adapter_up_query=adapter_up_query, adapter_up_key_value=adapter_up_key_value)


adapter_scale = 0.5
rope_base = 500000.0
epsilon = 1e-05

def normalize(hidden, attention_norm_gain):
    values = hidden.astype(jnp.float32)
    factor = lax.rsqrt(lax.optimization_barrier(jnp.mean(values * values, axis=-1, keepdims=True)) + epsilon)
    return (values * factor * attention_norm_gain.astype(jnp.float32)[None, :]).astype(jnp.bfloat16)

def rotate(vectors, positions):
    half_dim = vectors.shape[-1] // 2
    frequency = rope_base ** (-2.0 * jnp.arange(half_dim, dtype=jnp.float32) / vectors.shape[-1])
    angles = positions.astype(jnp.float32)[:, None] * frequency[None, :]
    cosine = jnp.cos(angles)[:, None, :]
    sine_part = jnp.sin(angles)[:, None, :]
    lower_half = vectors[..., :half_dim]
    upper_half = vectors[..., half_dim:]
    return jnp.concatenate([lower_half * cosine - upper_half * sine_part, upper_half * cosine + lower_half * sine_part], axis=-1)

def attend(queries, new_keys, new_values, paged_key_cache, paged_value_cache, lengths):
    factor = 1.0 / math.sqrt(queries.shape[-1])
    scores = jnp.einsum('rgqd,rgld->rgql', queries.astype(jnp.float32), paged_key_cache.astype(jnp.float32)) * factor
    own_score = jnp.einsum('rgqd,rgd->rgq', queries.astype(jnp.float32), new_keys.astype(jnp.float32)) * factor
    visible = jnp.arange(paged_key_cache.shape[2], dtype=jnp.int32)[None, None, None, :] < lengths[:, None, None, None]
    scores = jnp.where(visible, scores, -jnp.inf)
    row_max = jnp.maximum(lax.optimization_barrier(jnp.max(scores, axis=-1)), own_score)
    weights = jnp.exp(scores - row_max[..., None])
    own_weight = jnp.exp(own_score - row_max)
    denominator = lax.optimization_barrier(jnp.sum(weights, axis=-1)) + own_weight
    weights = (weights / denominator[..., None]).astype(jnp.bfloat16)
    own_weight = (own_weight / denominator).astype(jnp.bfloat16)
    attended = jnp.einsum('rgql,rgld->rgqd', weights.astype(jnp.float32), paged_value_cache.astype(jnp.float32))
    attended = attended + own_weight.astype(jnp.float32)[..., None] * new_values.astype(jnp.float32)[:, :, None, :]
    return attended.astype(jnp.bfloat16)

def reference(hidden, attention_norm_gain, row_adapter_index, lengths, paged_key_cache, paged_value_cache, query_weight, key_weight, value_weight, adapter_down_weight, adapter_up_query, adapter_up_key_value):
    normed = normalize(hidden, attention_norm_gain)
    base_products = jnp.concatenate([jnp.dot(normed, matrix, preferred_element_type=jnp.float32) for matrix in (query_weight, key_weight, value_weight)], axis=1)

    def one_row(pair_item):
        row_vec, adapter_slot = pair_item
        down_weight_rows = lax.dynamic_index_in_dim(adapter_down_weight, adapter_slot, 0, keepdims=False)
        rank_sums = jnp.einsum('prd,d->pr', down_weight_rows.astype(jnp.float32), row_vec.astype(jnp.float32)).astype(jnp.bfloat16)
        query_up_weight = lax.dynamic_index_in_dim(adapter_up_query, adapter_slot, 0, keepdims=False)
        key_value_up_weight = lax.dynamic_index_in_dim(adapter_up_key_value, adapter_slot, 0, keepdims=False)
        query_update = jnp.dot(rank_sums[0], query_up_weight, preferred_element_type=jnp.float32)
        key_update = jnp.dot(rank_sums[1], key_value_up_weight[0], preferred_element_type=jnp.float32)
        value_update = jnp.dot(rank_sums[2], key_value_up_weight[1], preferred_element_type=jnp.float32)
        return jnp.concatenate([query_update, key_update, value_update])
    adapter_updates = lax.map(one_row, (normed, row_adapter_index.astype(jnp.int32)))
    projected_rows = base_products + adapter_scale * adapter_updates
    row_count = hidden.shape[0]
    query_width = QUERY_HEADS * HEAD_WIDTH
    kv_width = KEY_VALUE_HEADS * HEAD_WIDTH
    queries = rotate(projected_rows[:, :query_width].reshape(row_count, QUERY_HEADS, HEAD_WIDTH), lengths).astype(jnp.bfloat16)
    new_keys = rotate(projected_rows[:, query_width:query_width + kv_width].reshape(row_count, KEY_VALUE_HEADS, HEAD_WIDTH), lengths).astype(jnp.bfloat16)
    new_values = projected_rows[:, query_width + kv_width:].reshape(row_count, KEY_VALUE_HEADS, HEAD_WIDTH).astype(jnp.bfloat16)
    grouped = queries.reshape(row_count, KEY_VALUE_HEADS, QUERY_HEADS // KEY_VALUE_HEADS, HEAD_WIDTH)
    attended = attend(grouped, new_keys, new_values, paged_key_cache, paged_value_cache, lengths)
    return attended.reshape(row_count, query_width)
```

```python
import functools
import math

import jax
import jax.numpy as jnp
from jax import lax
from jax.experimental import pallas as pl
from jax.experimental.pallas import tpu as pltpu
from jax.sharding import PartitionSpec as P

HEAD_WIDTH = 128
LANES = 128

adapter_scale = 0.5
rope_base = 500000.0
epsilon = 1e-05

RING = (0, 1, 2, 3)
XOR = False
N_ORDER = (1, 2, 3)
W_ORDER = (1, 2, 3)
O_ORDER = (2, 1, 3)

f32 = jnp.float32
bf16 = jnp.bfloat16

VMEM = pl.BlockSpec(memory_space=pltpu.VMEM)
ANY = pl.BlockSpec(memory_space=pl.ANY)
HBM = pl.BlockSpec(memory_space=pltpu.HBM)


def shape_of(shape, dtype):
    return jax.ShapeDtypeStruct(shape, dtype)


def call(kernel, outs, in_specs, args, scratch=(), flops=0, nbytes=0, vmem=8):
    return pl.pallas_call(
        kernel,
        out_shape=outs,
        in_specs=in_specs,
        out_specs=jax.tree.map(lambda _: VMEM, outs),
        scratch_shapes=scratch,
        compiler_params=pltpu.CompilerParams(vmem_limit_bytes=vmem * 2**20),
        cost_estimate=pl.CostEstimate(flops=flops, bytes_accessed=nbytes, transcendentals=0),
    )(*args)


def own_place():
    return lax.axis_index("wide"), lax.axis_index("narrow")


def normalize_kernel(wide, index_far, hidden_far, gain_far, message, *refs):
    slices, (scratch, index, hidden, gain, sems) = refs[:wide], refs[wide:]
    copies = [
        pltpu.make_async_copy(far, near, sems.at[i])
        for i, (far, near) in enumerate(
            ((hidden_far, hidden), (gain_far, gain), (index_far, index))
        )
    ]
    for copy in copies:
        copy.start()
    wide_place, narrow_place = own_place()
    rows = hidden.shape[0]
    half = message.shape[1] - LANES
    wide_half = slices[0].shape[1]
    copies[0].wait()
    values = hidden[...].astype(f32)
    factor = lax.rsqrt(jnp.mean(values * values, axis=-1, keepdims=True) + epsilon)
    copies[1].wait()
    copies[2].wait()
    scale = gain[...].astype(f32).reshape(1, -1)
    normed = (values * factor * scale).astype(bf16)
    scratch[...] = normed.astype(f32)

    def stacked(start, width):
        return jnp.concatenate(
            [
                scratch[:, pl.ds(pl.multiple_of(start, LANES), width)],
                scratch[:, pl.ds(pl.multiple_of(start + width, LANES), width)],
            ],
            axis=0,
        ).astype(bf16)

    message[:, :half] = stacked(narrow_place * (2 * half), half)
    row = lax.broadcasted_iota(jnp.int32, (2 * rows, LANES), 0)
    ids = jnp.zeros((2 * rows, LANES), f32)
    for r in range(rows):
        ids = jnp.where((row == r) | (row == r + rows), index[r].astype(f32), ids)
    message[:, half:] = ids.astype(bf16)
    for k in range(wide):
        target = after(wide_place, k, wide)
        slices[k][...] = stacked(target * (2 * wide_half), wide_half)


def joined(blocks):
    rows = blocks[0].shape[0] // 2
    values = [block[...].astype(f32) for block in blocks]
    upper = jnp.concatenate([value[:rows] for value in values], axis=0)
    lower = jnp.concatenate([value[rows:] for value in values], axis=0)
    return upper, lower


def down_kernel(wide, rank3, *refs):
    blocks, down, (sums, ids) = refs[:wide], refs[wide], refs[wide + 1 :]
    wide_place, _ = own_place()
    count = down.shape[0] // rank3
    upper, lower = joined(restored(blocks, N_ORDER))
    half = upper.shape[1] - LANES
    row_ids = upper[:, half:]
    ids[...] = row_ids
    features = jnp.concatenate([upper[:, :half], lower[:, :half]], axis=1).astype(bf16)
    first = wide_place * count
    total = jnp.zeros((features.shape[0], rank3), f32)
    for e in range(count):
        product = lax.dot_general(
            features,
            down[e * rank3 : (e + 1) * rank3, :],
            (((1,), (1,)), ((), ())),
            preferred_element_type=f32,
        )
        total = jnp.where(row_ids[:, :1] == (first + e).astype(f32), product, total)
    sums[...] = total


def base_kernel(wide, *refs):
    blocks, sources, out = refs[:wide], refs[wide:-1], refs[-1]
    chunk = 256
    upper, lower = (part.astype(bf16) for part in joined(restored(blocks, W_ORDER)))
    half = upper.shape[1]
    offset = 0
    for source in sources:
        for start in range(0, source.shape[1], chunk):
            columns = slice(start, start + chunk)
            out[:, offset + start : offset + start + chunk] = jnp.dot(
                upper, source[:half, columns], preferred_element_type=f32
            ) + jnp.dot(lower, source[half:, columns], preferred_element_type=f32)
        offset += source.shape[1]


LARGEST = 32767.0
STEP_ROWS = 16


def step_of(exponent):
    return jnp.exp2(exponent * 0.25) * (1.0 / LARGEST)


def up_kernel(wide, narrow, base, ids, *refs):
    parts, (query_up, pair_up) = refs[:narrow], refs[narrow : narrow + 2]
    own, *outs = refs[narrow + 2 : narrow + 2 + wide]
    sums, codes = refs[narrow + 2 + wide :]
    wide_place, _ = own_place()
    count, _, rank, pair_width = pair_up.shape
    all_rows, width = base.shape
    rows = all_rows // wide
    total = parts[0][...]
    for part in parts[1:]:
        total = total + part[...]
    rank_sums = total.astype(bf16)
    row_ids = ids[:, :1]
    first = wide_place * count

    def widen(p):
        piece = rank_sums[:, p * rank : (p + 1) * rank].astype(f32)
        return jnp.concatenate(
            [jnp.where(row_ids == (first + e).astype(f32), piece, 0.0) for e in range(count)],
            axis=1,
        ).astype(bf16)

    chunk = 256
    query_width = query_up.shape[1]
    pairs = [
        jnp.concatenate([pair_up[e, p] for e in range(count)], axis=0) for p in range(2)
    ]
    groups = (
        (widen(0), query_up, 0, query_width),
        (widen(1), pairs[0], query_width, pair_width),
        (widen(2), pairs[1], query_width + pair_width, pair_width),
    )
    exponents = []
    for lhs, weights, offset, group_width in groups:
        top = jnp.zeros((all_rows, LANES), f32)
        for start in range(0, group_width, chunk):
            columns = slice(offset + start, offset + start + chunk)
            values = base[:, columns] + adapter_scale * jnp.dot(
                lhs, weights[:, start : start + chunk], preferred_element_type=f32
            )
            sums[:, columns] = values
            for j in range(0, chunk, LANES):
                top = jnp.maximum(top, jnp.abs(values[:, j : j + LANES]))
        top = jnp.maximum(jnp.max(top, axis=-1, keepdims=True), 1e-30)
        exponents.append(jnp.ceil(4.0 * jnp.log2(top) + 0.01))
    for (_, _, offset, group_width), exponent in zip(groups, exponents):
        inverse = 1.0 / step_of(exponent)
        for start in range(offset, offset + group_width, LANES):
            values = sums[:, start : start + LANES]
            window = slice(start // LANES * rows, (start // LANES + 1) * rows)
            own[window, :] = values[:rows]
            rounded = jnp.round(values * inverse)
            for k in range(1, wide):
                codes[k - 1, window, :] = rounded[k * rows : (k + 1) * rows]
    lane = lax.broadcasted_iota(jnp.int32, (all_rows, LANES), 1)
    marks = jnp.where(
        lane < 32, exponents[0], jnp.where(lane < 64, exponents[1], exponents[2])
    )
    body = width // LANES * rows
    rest = jnp.zeros((outs[0].shape[0] - body - rows, LANES), f32)
    for k in range(1, wide):
        mark = jnp.concatenate([marks[k * rows : (k + 1) * rows], rest], axis=0)
        outs[k - 1][:body, :] = codes[k - 1].astype(jnp.int32).astype(jnp.int16)
        outs[k - 1][body:, :] = mark.astype(jnp.int32).astype(jnp.int16)


def attend_kernel(wide, heads, kv_heads, visible, cosine, sine, *refs):
    parts, (keys, values, out, rotated, attended) = refs[:wide], refs[wide:]
    rows, _, _, width = keys.shape
    group = heads // kv_heads
    body = (heads + 2 * kv_heads) * rows
    total = parts[0][...]
    for part in parts[1:]:
        steps = step_of(part[body:, :].astype(jnp.int32).astype(f32)[:rows])
        query_step, key_step, value_step = (
            jnp.broadcast_to(steps[:, lane : lane + 1], (rows, width)) for lane in (0, 32, 64)
        )
        step = jnp.concatenate(
            [query_step] * heads + [key_step] * kv_heads + [value_step] * kv_heads, axis=0
        )
        total = total + part[:body, :].astype(jnp.int32).astype(f32) * step
    turned = (heads + kv_heads) * rows
    straight = total[:turned]
    straight = straight * cosine[...] + pltpu.roll(straight, width // 2, 1) * sine[...]
    rotated[:turned] = straight.astype(bf16).astype(f32)
    rotated[turned:] = total[turned:].astype(bf16).astype(f32)
    factor = 1.0 / math.sqrt(width)
    pairs = [(r, g) for r in range(rows) for g in range(kv_heads)]
    scores, own = [], []
    for r, g in pairs:
        query = rotated[pl.ds(g * group * rows + r, group, stride=rows), :]
        new_key = rotated[pl.ds((heads + g) * rows + r, 1), :]
        score = lax.dot_general(
            query.astype(bf16), keys[r, g], (((1,), (1,)), ((), ())), preferred_element_type=f32
        )
        scores.append(score * factor + visible[r : r + 1, :])
        own.append(jnp.sum(query * new_key, axis=-1, keepdims=True) * factor)
    score, own = jnp.concatenate(scores, axis=0), jnp.concatenate(own, axis=0)
    row_max = jnp.maximum(jnp.max(score, axis=-1, keepdims=True), own)
    weights = jnp.exp(score - row_max)
    own_weight = jnp.exp(own - row_max)
    denominator = jnp.sum(weights, axis=-1, keepdims=True) + own_weight
    weights = (weights / denominator).astype(bf16)
    own_weight = (own_weight / denominator).astype(bf16).astype(f32)
    mixed = []
    for i, (r, g) in enumerate(pairs):
        new_value = rotated[pl.ds((heads + kv_heads + g) * rows + r, 1), :]
        window = slice(i * group, (i + 1) * group)
        mixed.append(
            jnp.dot(weights[window], values[r, g], preferred_element_type=f32)
            + own_weight[window] * new_value
        )
    for i, (r, g) in enumerate(pairs):
        attended[pl.ds(g * group * rows + r, group, stride=rows), :] = mixed[i]
    for h in range(heads):
        out[:, h * width : (h + 1) * width] = attended[h * rows : (h + 1) * rows, :].astype(bf16)


def rotation_kernel(lengths_far, after, cosine, sine, visible, lengths, sem):
    copy = pltpu.make_async_copy(lengths_far, lengths, sem)
    copy.start()
    rows, positions = visible.shape
    half_dim = HEAD_WIDTH // 2
    lane = lax.broadcasted_iota(jnp.int32, (rows, HEAD_WIDTH), 1)
    place = jnp.where(lane < half_dim, lane, lane - half_dim).astype(f32)
    frequency = jnp.exp(place * (-2.0 / HEAD_WIDTH * math.log(rope_base)))
    row = lax.broadcasted_iota(jnp.int32, (rows, positions), 0)
    length = jnp.zeros((rows, positions), jnp.int32)
    copy.wait()
    for r in range(rows):
        length = jnp.where(row == r, lengths[r], length)
    position = lax.broadcasted_iota(jnp.int32, (rows, positions), 1)
    visible[...] = jnp.where(position < length, 0.0, -jnp.inf)
    angles = length[:, :HEAD_WIDTH].astype(f32) * frequency
    cosines = jnp.cos(angles)
    sines = jnp.where(lane < half_dim, -1.0, 1.0) * jnp.sin(angles)
    repeats = cosine.shape[0] // rows
    cosine[...] = jnp.concatenate([cosines] * repeats, axis=0)
    sine[...] = jnp.concatenate([sines] * repeats, axis=0)


def arranged(order, count):
    return [k for k in order if k < count] + [k for k in range(1, count) if k not in order]


def restored(items, order):
    order = arranged(order, len(items))
    return [items[0]] + [items[1 + order.index(k)] for k in range(1, len(items))]


def shifted(count, k):
    return [(i, (i + k) % count) for i in range(count)]


def ring_of(count):
    return RING if len(RING) == count else tuple(range(count))


def after(place, k, count):
    if XOR:
        return place ^ k
    ring = ring_of(count)
    if ring == tuple(range(count)):
        return lax.rem(place + k, count) if not isinstance(place, int) else (place + k) % count
    if isinstance(place, int):
        return ring[(ring.index(place) + k) % count]
    result = jnp.int32(0)
    for i in range(count):
        result = jnp.where(place == i, after(i, k, count), result)
    return result


def ringed(count, k):
    return [(i, after(i, k % count, count)) for i in range(count)]


def on_device(
    hidden,
    attention_norm_gain,
    row_adapter_index,
    lengths,
    paged_key_cache,
    paged_value_cache,
    query_weight,
    key_weight,
    value_weight,
    adapter_down_weight,
    adapter_up_query,
    adapter_up_key_value,
):
    wide, narrow = lax.axis_size("wide"), lax.axis_size("narrow")
    rows, features = hidden.shape
    count, _, rank, slice_width = adapter_down_weight.shape
    query_width, kv_width = query_weight.shape[1], key_weight.shape[1]
    heads, kv_heads = query_width // HEAD_WIDTH, kv_width // HEAD_WIDTH
    all_rows = rows * wide
    rank3 = 3 * rank
    width = query_width + 2 * kv_width
    half, wide_half = slice_width // 2, query_weight.shape[0] // 2

    message, *slices = call(
        functools.partial(normalize_kernel, wide),
        [shape_of((2 * rows, half + LANES), bf16)] + [shape_of((2 * rows, wide_half), bf16)] * wide,
        [HBM, HBM, HBM],
        [
            pltpu.with_memory_space_constraint(x, pltpu.HBM)
            for x in (row_adapter_index, hidden, attention_norm_gain)
        ],
        [
            pltpu.VMEM((rows, features), f32),
            pltpu.SMEM((rows,), jnp.int32),
            pltpu.VMEM((rows, features), bf16),
            pltpu.VMEM((features,), bf16),
            pltpu.SemaphoreType.DMA((3,)),
        ],
        flops=10**10,
    )
    blocks = [message] + [
        lax.ppermute(message, "wide", ringed(wide, k)) for k in arranged(N_ORDER, wide)
    ]
    wide_blocks = [slices[0]] + [
        lax.ppermute(slices[k], "wide", ringed(wide, k)) for k in arranged(W_ORDER, wide)
    ]
    down = adapter_down_weight.reshape(count * rank3, slice_width)
    sums, ids = call(
        functools.partial(down_kernel, wide, rank3),
        [shape_of((all_rows, rank3), f32), shape_of((all_rows, LANES), f32)],
        [VMEM] * wide + [VMEM],
        (*blocks, down),
        vmem=12,
        flops=2 * all_rows * down.size,
        nbytes=2 * down.size,
    )
    parts = [sums] + [lax.ppermute(sums, "narrow", shifted(narrow, k)) for k in range(1, narrow)]
    weights = (query_weight, key_weight, value_weight)
    base = call(
        functools.partial(base_kernel, wide),
        shape_of((all_rows, width), f32),
        [VMEM] * wide + [VMEM] * 3,
        (*wide_blocks, *weights),
        vmem=16,
        flops=4 * all_rows * width * wide_half,
        nbytes=4 * width * wide_half,
    )
    query_up = adapter_up_query.reshape(count * rank, query_width)
    body = width // LANES * rows
    step_rows = -(-rows // STEP_ROWS) * STEP_ROWS
    outs = call(
        functools.partial(up_kernel, wide, narrow),
        [shape_of((body, LANES), f32)]
        + [shape_of((body + step_rows, LANES), jnp.int16)] * (wide - 1),
        [VMEM, VMEM] + [VMEM] * narrow + [VMEM] * 2,
        (base, ids, *parts, query_up, adapter_up_key_value),
        [pltpu.VMEM((all_rows, width), f32), pltpu.VMEM((wide - 1, body, LANES), f32)],
        vmem=10 + wide // 2,
        flops=2 * all_rows * width * count * rank,
        nbytes=2 * width * count * rank,
    )
    gathered = [outs[0]] + [
        lax.ppermute(outs[k], "wide", ringed(wide, k if XOR else -k)) for k in arranged(O_ORDER, wide)
    ]
    turned = (heads + kv_heads) * rows
    cosine, sine, visible = call(
        rotation_kernel,
        [shape_of((turned, LANES), f32)] * 2 + [shape_of((rows, paged_key_cache.shape[2]), f32)],
        [HBM, ANY],
        (pltpu.with_memory_space_constraint(lengths, pltpu.HBM), outs[0]),
        [pltpu.SMEM((rows,), jnp.int32), pltpu.SemaphoreType.DMA],
    )
    return call(
        functools.partial(attend_kernel, wide, heads, kv_heads),
        shape_of((rows, query_width), bf16),
        [VMEM] * (3 + wide + 2),
        (visible, cosine, sine, *gathered, paged_key_cache, paged_value_cache),
        [
            pltpu.VMEM((body, LANES), f32),
            pltpu.VMEM((heads * rows, LANES), f32),
        ],
        vmem=8 + wide // 4,
        flops=4 * paged_key_cache.size * 8,
        nbytes=4 * paged_key_cache.size,
    )


def solution(mesh):
    in_specs = (
        P(("groups", "wide"), None),
        P(),
        P(("groups", "wide")),
        P(("groups", "wide")),
        P(("groups", "wide"), "narrow", None, None),
        P(("groups", "wide"), "narrow", None, None),
        P("wide", "narrow"),
        P("wide", "narrow"),
        P("wide", "narrow"),
        P(("groups", "wide"), None, None, "narrow"),
        P(("groups", "wide"), None, "narrow"),
        P(("groups", "wide"), None, None, "narrow"),
    )
    out_specs = P(("groups", "wide"), "narrow")
    return jax.shard_map(
        on_device, mesh=mesh, in_specs=in_specs, out_specs=out_specs, check_vma=False
    )
```

```python
import functools
import math

import jax
import jax.numpy as jnp
from jax import lax
from jax.experimental import pallas as pl
from jax.experimental.pallas import tpu as pltpu
from jax.sharding import PartitionSpec as P

HEAD_WIDTH = 128
LANES = 128

adapter_scale = 0.5
rope_base = 500000.0
epsilon = 1e-05

LAST_ORDER = (2, 3, 1)

f32 = jnp.float32
bf16 = jnp.bfloat16

VMEM = pl.BlockSpec(memory_space=pltpu.VMEM)
ANY = pl.BlockSpec(memory_space=pl.ANY)
HBM = pl.BlockSpec(memory_space=pltpu.HBM)


def shape_of(shape, dtype):
    return jax.ShapeDtypeStruct(shape, dtype)


def call(kernel, outs, in_specs, args, scratch=(), flops=0, nbytes=0, vmem=8):
    return pl.pallas_call(
        kernel,
        out_shape=outs,
        in_specs=in_specs,
        out_specs=jax.tree.map(lambda _: VMEM, outs),
        scratch_shapes=scratch,
        compiler_params=pltpu.CompilerParams(vmem_limit_bytes=vmem * 2**20),
        cost_estimate=pl.CostEstimate(flops=flops, bytes_accessed=nbytes, transcendentals=0),
    )(*args)


def own_place():
    return lax.axis_index("wide"), lax.axis_index("narrow")


def normalize_kernel(wide, index_far, hidden_far, gain_far, message, *refs):
    slices, (scratch, index, hidden, gain, sems) = refs[:wide], refs[wide:]
    copies = [
        pltpu.make_async_copy(far, near, sems.at[i])
        for i, (far, near) in enumerate(
            ((hidden_far, hidden), (gain_far, gain), (index_far, index))
        )
    ]
    for copy in copies:
        copy.start()
    wide_place, narrow_place = own_place()
    rows = hidden.shape[0]
    half = message.shape[1] - LANES
    wide_half = slices[0].shape[1]
    copies[0].wait()
    values = hidden[...].astype(f32)
    factor = lax.rsqrt(jnp.mean(values * values, axis=-1, keepdims=True) + epsilon)
    copies[1].wait()
    copies[2].wait()
    scale = gain[...].astype(f32).reshape(1, -1)
    normed = (values * factor * scale).astype(bf16)
    scratch[...] = normed.astype(f32)

    def stacked(start, width):
        return jnp.concatenate(
            [
                scratch[:, pl.ds(pl.multiple_of(start, LANES), width)],
                scratch[:, pl.ds(pl.multiple_of(start + width, LANES), width)],
            ],
            axis=0,
        ).astype(bf16)

    message[:, :half] = stacked(narrow_place * (2 * half), half)
    row = lax.broadcasted_iota(jnp.int32, (2 * rows, LANES), 0)
    ids = jnp.zeros((2 * rows, LANES), f32)
    for r in range(rows):
        ids = jnp.where((row == r) | (row == r + rows), index[r].astype(f32), ids)
    message[:, half:] = ids.astype(bf16)
    for k in range(wide):
        target = lax.bitwise_xor(wide_place, k)
        slices[k][...] = stacked(target * (2 * wide_half), wide_half)


def joined(blocks):
    rows = blocks[0].shape[0] // 2
    values = [block[...].astype(f32) for block in blocks]
    upper = jnp.concatenate([value[:rows] for value in values], axis=0)
    lower = jnp.concatenate([value[rows:] for value in values], axis=0)
    return upper, lower


def down_kernel(wide, rank3, *refs):
    blocks, down, (sums, ids) = refs[:wide], refs[wide], refs[wide + 1 :]
    wide_place, _ = own_place()
    count = down.shape[0] // rank3
    upper, lower = joined(blocks)
    half = upper.shape[1] - LANES
    row_ids = upper[:, half:]
    ids[...] = row_ids
    features = jnp.concatenate([upper[:, :half], lower[:, :half]], axis=1).astype(bf16)
    first = wide_place * count
    total = jnp.zeros((features.shape[0], rank3), f32)
    for e in range(count):
        product = lax.dot_general(
            features,
            down[e * rank3 : (e + 1) * rank3, :],
            (((1,), (1,)), ((), ())),
            preferred_element_type=f32,
        )
        total = jnp.where(row_ids[:, :1] == (first + e).astype(f32), product, total)
    sums[...] = total


def base_kernel(wide, *refs):
    blocks, sources, out = refs[:wide], refs[wide:-1], refs[-1]
    chunk = 256
    upper, lower = (part.astype(bf16) for part in joined(blocks))
    half = upper.shape[1]
    offset = 0
    for source in sources:
        for start in range(0, source.shape[1], chunk):
            columns = slice(start, start + chunk)
            out[:, offset + start : offset + start + chunk] = jnp.dot(
                upper, source[:half, columns], preferred_element_type=f32
            ) + jnp.dot(lower, source[half:, columns], preferred_element_type=f32)
        offset += source.shape[1]


LARGEST = 32767.0
STEP_ROWS = 16


def step_of(exponent):
    return jnp.exp2(exponent * 0.25) * (1.0 / LARGEST)


def up_kernel(wide, narrow, base, ids, *refs):
    parts, (query_up, pair_up) = refs[:narrow], refs[narrow : narrow + 2]
    own, *outs = refs[narrow + 2 : narrow + 2 + wide]
    sums, codes = refs[narrow + 2 + wide :]
    wide_place, _ = own_place()
    count, _, rank, pair_width = pair_up.shape
    all_rows, width = base.shape
    rows = all_rows // wide
    total = parts[0][...]
    for part in parts[1:]:
        total = total + part[...]
    rank_sums = total.astype(bf16)
    row_ids = ids[:, :1]
    first = wide_place * count

    def widen(p):
        piece = rank_sums[:, p * rank : (p + 1) * rank].astype(f32)
        return jnp.concatenate(
            [jnp.where(row_ids == (first + e).astype(f32), piece, 0.0) for e in range(count)],
            axis=1,
        ).astype(bf16)

    chunk = 256
    query_width = query_up.shape[1]
    pairs = [
        jnp.concatenate([pair_up[e, p] for e in range(count)], axis=0) for p in range(2)
    ]
    groups = (
        (widen(0), query_up, 0, query_width),
        (widen(1), pairs[0], query_width, pair_width),
        (widen(2), pairs[1], query_width + pair_width, pair_width),
    )
    exponents = []
    for lhs, weights, offset, group_width in groups:
        top = jnp.zeros((all_rows, LANES), f32)
        for start in range(0, group_width, chunk):
            columns = slice(offset + start, offset + start + chunk)
            values = base[:, columns] + adapter_scale * jnp.dot(
                lhs, weights[:, start : start + chunk], preferred_element_type=f32
            )
            sums[:, columns] = values
            for j in range(0, chunk, LANES):
                top = jnp.maximum(top, jnp.abs(values[:, j : j + LANES]))
        top = jnp.maximum(jnp.max(top, axis=-1, keepdims=True), 1e-30)
        exponents.append(jnp.ceil(4.0 * jnp.log2(top) + 0.01))
    for (_, _, offset, group_width), exponent in zip(groups, exponents):
        inverse = 1.0 / step_of(exponent)
        for start in range(offset, offset + group_width, LANES):
            values = sums[:, start : start + LANES]
            window = slice(start // LANES * rows, (start // LANES + 1) * rows)
            own[window, :] = values[:rows]
            rounded = jnp.round(values * inverse)
            for k in range(1, wide):
                codes[k - 1, window, :] = rounded[k * rows : (k + 1) * rows]
    lane = lax.broadcasted_iota(jnp.int32, (all_rows, LANES), 1)
    marks = jnp.where(
        lane < 32, exponents[0], jnp.where(lane < 64, exponents[1], exponents[2])
    )
    body = width // LANES * rows
    rest = jnp.zeros((outs[0].shape[0] - body - rows, LANES), f32)
    for k in range(1, wide):
        mark = jnp.concatenate([marks[k * rows : (k + 1) * rows], rest], axis=0)
        outs[k - 1][:body, :] = codes[k - 1].astype(jnp.int32).astype(jnp.int16)
        outs[k - 1][body:, :] = mark.astype(jnp.int32).astype(jnp.int16)


def attend_kernel(wide, heads, kv_heads, visible, cosine, sine, *refs):
    parts, (keys, values, out, rotated, attended) = refs[:wide], refs[wide:]
    rows, _, _, width = keys.shape
    group = heads // kv_heads
    body = (heads + 2 * kv_heads) * rows
    total = parts[0][...]
    for part in parts[1:]:
        steps = step_of(part[body:, :].astype(jnp.int32).astype(f32)[:rows])
        query_step, key_step, value_step = (
            jnp.broadcast_to(steps[:, lane : lane + 1], (rows, width)) for lane in (0, 32, 64)
        )
        step = jnp.concatenate(
            [query_step] * heads + [key_step] * kv_heads + [value_step] * kv_heads, axis=0
        )
        total = total + part[:body, :].astype(jnp.int32).astype(f32) * step
    turned = (heads + kv_heads) * rows
    straight = total[:turned]
    straight = straight * cosine[...] + pltpu.roll(straight, width // 2, 1) * sine[...]
    rotated[:turned] = straight.astype(bf16).astype(f32)
    rotated[turned:] = total[turned:].astype(bf16).astype(f32)
    factor = 1.0 / math.sqrt(width)
    pairs = [(r, g) for r in range(rows) for g in range(kv_heads)]
    scores, own = [], []
    for r, g in pairs:
        query = rotated[pl.ds(g * group * rows + r, group, stride=rows), :]
        new_key = rotated[pl.ds((heads + g) * rows + r, 1), :]
        score = lax.dot_general(
            query.astype(bf16), keys[r, g], (((1,), (1,)), ((), ())), preferred_element_type=f32
        )
        scores.append(score * factor + visible[r : r + 1, :])
        own.append(jnp.sum(query * new_key, axis=-1, keepdims=True) * factor)
    score, own = jnp.concatenate(scores, axis=0), jnp.concatenate(own, axis=0)
    row_max = jnp.maximum(jnp.max(score, axis=-1, keepdims=True), own)
    weights = jnp.exp(score - row_max)
    own_weight = jnp.exp(own - row_max)
    denominator = jnp.sum(weights, axis=-1, keepdims=True) + own_weight
    weights = (weights / denominator).astype(bf16)
    own_weight = (own_weight / denominator).astype(bf16).astype(f32)
    mixed = []
    for i, (r, g) in enumerate(pairs):
        new_value = rotated[pl.ds((heads + kv_heads + g) * rows + r, 1), :]
        window = slice(i * group, (i + 1) * group)
        mixed.append(
            jnp.dot(weights[window], values[r, g], preferred_element_type=f32)
            + own_weight[window] * new_value
        )
    for i, (r, g) in enumerate(pairs):
        attended[pl.ds(g * group * rows + r, group, stride=rows), :] = mixed[i]
    for h in range(heads):
        out[:, h * width : (h + 1) * width] = attended[h * rows : (h + 1) * rows, :].astype(bf16)


def rotation_kernel(lengths_far, after, cosine, sine, visible, lengths, sem):
    copy = pltpu.make_async_copy(lengths_far, lengths, sem)
    copy.start()
    rows, positions = visible.shape
    half_dim = HEAD_WIDTH // 2
    lane = lax.broadcasted_iota(jnp.int32, (rows, HEAD_WIDTH), 1)
    place = jnp.where(lane < half_dim, lane, lane - half_dim).astype(f32)
    frequency = jnp.exp(place * (-2.0 / HEAD_WIDTH * math.log(rope_base)))
    row = lax.broadcasted_iota(jnp.int32, (rows, positions), 0)
    length = jnp.zeros((rows, positions), jnp.int32)
    copy.wait()
    for r in range(rows):
        length = jnp.where(row == r, lengths[r], length)
    position = lax.broadcasted_iota(jnp.int32, (rows, positions), 1)
    visible[...] = jnp.where(position < length, 0.0, -jnp.inf)
    angles = length[:, :HEAD_WIDTH].astype(f32) * frequency
    cosines = jnp.cos(angles)
    sines = jnp.where(lane < half_dim, -1.0, 1.0) * jnp.sin(angles)
    repeats = cosine.shape[0] // rows
    cosine[...] = jnp.concatenate([cosines] * repeats, axis=0)
    sine[...] = jnp.concatenate([sines] * repeats, axis=0)


def shifted(count, k):
    return [(i, (i + k) % count) for i in range(count)]


def paired(count, k):
    return [(i, i ^ k) for i in range(count)]


def on_device(
    hidden,
    attention_norm_gain,
    row_adapter_index,
    lengths,
    paged_key_cache,
    paged_value_cache,
    query_weight,
    key_weight,
    value_weight,
    adapter_down_weight,
    adapter_up_query,
    adapter_up_key_value,
):
    wide, narrow = lax.axis_size("wide"), lax.axis_size("narrow")
    rows, features = hidden.shape
    count, _, rank, slice_width = adapter_down_weight.shape
    query_width, kv_width = query_weight.shape[1], key_weight.shape[1]
    heads, kv_heads = query_width // HEAD_WIDTH, kv_width // HEAD_WIDTH
    all_rows = rows * wide
    rank3 = 3 * rank
    width = query_width + 2 * kv_width
    half, wide_half = slice_width // 2, query_weight.shape[0] // 2

    message, *slices = call(
        functools.partial(normalize_kernel, wide),
        [shape_of((2 * rows, half + LANES), bf16)] + [shape_of((2 * rows, wide_half), bf16)] * wide,
        [HBM, HBM, HBM],
        [
            pltpu.with_memory_space_constraint(x, pltpu.HBM)
            for x in (row_adapter_index, hidden, attention_norm_gain)
        ],
        [
            pltpu.VMEM((rows, features), f32),
            pltpu.SMEM((rows,), jnp.int32),
            pltpu.VMEM((rows, features), bf16),
            pltpu.VMEM((features,), bf16),
            pltpu.SemaphoreType.DMA((3,)),
        ],
        flops=10**10,
    )
    blocks = [message] + [
        lax.ppermute(message, "wide", paired(wide, k)) for k in range(1, wide)
    ]
    wide_blocks = [slices[0]] + [
        lax.ppermute(slices[k], "wide", paired(wide, k)) for k in range(1, wide)
    ]
    down = adapter_down_weight.reshape(count * rank3, slice_width)
    sums, ids = call(
        functools.partial(down_kernel, wide, rank3),
        [shape_of((all_rows, rank3), f32), shape_of((all_rows, LANES), f32)],
        [VMEM] * wide + [VMEM],
        (*blocks, down),
        vmem=12,
        flops=2 * all_rows * down.size,
        nbytes=2 * down.size,
    )
    parts = [sums] + [lax.ppermute(sums, "narrow", shifted(narrow, k)) for k in range(1, narrow)]
    weights = (query_weight, key_weight, value_weight)
    base = call(
        functools.partial(base_kernel, wide),
        shape_of((all_rows, width), f32),
        [VMEM] * wide + [VMEM] * 3,
        (*wide_blocks, *weights),
        vmem=16,
        flops=4 * all_rows * width * wide_half,
        nbytes=4 * width * wide_half,
    )
    query_up = adapter_up_query.reshape(count * rank, query_width)
    body = width // LANES * rows
    step_rows = -(-rows // STEP_ROWS) * STEP_ROWS
    outs = call(
        functools.partial(up_kernel, wide, narrow),
        [shape_of((body, LANES), f32)]
        + [shape_of((body + step_rows, LANES), jnp.int16)] * (wide - 1),
        [VMEM, VMEM] + [VMEM] * narrow + [VMEM] * 2,
        (base, ids, *parts, query_up, adapter_up_key_value),
        [pltpu.VMEM((all_rows, width), f32), pltpu.VMEM((wide - 1, body, LANES), f32)],
        vmem=10 + wide // 2,
        flops=2 * all_rows * width * count * rank,
        nbytes=2 * width * count * rank,
    )
    gathered = [outs[0]] + [
        lax.ppermute(outs[k], "wide", paired(wide, k))
        for k in (LAST_ORDER if wide == 4 else range(1, wide))
    ]
    turned = (heads + kv_heads) * rows
    cosine, sine, visible = call(
        rotation_kernel,
        [shape_of((turned, LANES), f32)] * 2 + [shape_of((rows, paged_key_cache.shape[2]), f32)],
        [HBM, ANY],
        (pltpu.with_memory_space_constraint(lengths, pltpu.HBM), outs[0]),
        [pltpu.SMEM((rows,), jnp.int32), pltpu.SemaphoreType.DMA],
    )
    return call(
        functools.partial(attend_kernel, wide, heads, kv_heads),
        shape_of((rows, query_width), bf16),
        [VMEM] * (3 + wide + 2),
        (visible, cosine, sine, *gathered, paged_key_cache, paged_value_cache),
        [
            pltpu.VMEM((body, LANES), f32),
            pltpu.VMEM((heads * rows, LANES), f32),
        ],
        vmem=8 + wide // 4,
        flops=4 * paged_key_cache.size * 8,
        nbytes=4 * paged_key_cache.size,
    )


def solution(mesh):
    in_specs = (
        P(("groups", "wide"), None),
        P(),
        P(("groups", "wide")),
        P(("groups", "wide")),
        P(("groups", "wide"), "narrow", None, None),
        P(("groups", "wide"), "narrow", None, None),
        P("wide", "narrow"),
        P("wide", "narrow"),
        P("wide", "narrow"),
        P(("groups", "wide"), None, None, "narrow"),
        P(("groups", "wide"), None, "narrow"),
        P(("groups", "wide"), None, None, "narrow"),
    )
    out_specs = P(("groups", "wide"), "narrow")
    return jax.shard_map(
        on_device, mesh=mesh, in_specs=in_specs, out_specs=out_specs, check_vma=False
    )
```

```python
import functools
import math

import jax
import jax.numpy as jnp
from jax import lax
from jax.experimental import pallas as pl
from jax.experimental.pallas import tpu as pltpu
from jax.sharding import PartitionSpec as P

HEAD_WIDTH = 128
LANES = 128

adapter_scale = 0.5
rope_base = 500000.0
epsilon = 1e-05

LAST_ORDER = (2, 3, 1)

f32 = jnp.float32
bf16 = jnp.bfloat16

VMEM = pl.BlockSpec(memory_space=pltpu.VMEM)
ANY = pl.BlockSpec(memory_space=pl.ANY)
HBM = pl.BlockSpec(memory_space=pltpu.HBM)


def shape_of(shape, dtype):
    return jax.ShapeDtypeStruct(shape, dtype)


def call(kernel, outs, in_specs, args, scratch=(), flops=0, nbytes=0, vmem=8):
    return pl.pallas_call(
        kernel,
        out_shape=outs,
        in_specs=in_specs,
        out_specs=jax.tree.map(lambda _: VMEM, outs),
        scratch_shapes=scratch,
        compiler_params=pltpu.CompilerParams(vmem_limit_bytes=vmem * 2**20),
        cost_estimate=pl.CostEstimate(flops=flops, bytes_accessed=nbytes, transcendentals=0),
    )(*args)


def own_place():
    return lax.axis_index("wide"), lax.axis_index("narrow")


def normalize_kernel(wide, index_far, hidden_far, gain_far, message, *refs):
    slices, (scratch, index, hidden, gain, sems) = refs[:wide], refs[wide:]
    copies = [
        pltpu.make_async_copy(far, near, sems.at[i])
        for i, (far, near) in enumerate(
            ((hidden_far, hidden), (gain_far, gain), (index_far, index))
        )
    ]
    for copy in copies:
        copy.start()
    wide_place, narrow_place = own_place()
    rows = hidden.shape[0]
    half = message.shape[1] - LANES
    wide_half = slices[0].shape[1]
    copies[0].wait()
    values = hidden[...].astype(f32)
    factor = lax.rsqrt(jnp.mean(values * values, axis=-1, keepdims=True) + epsilon)
    copies[1].wait()
    copies[2].wait()
    scale = gain[...].astype(f32).reshape(1, -1)
    normed = (values * factor * scale).astype(bf16)
    scratch[...] = normed.astype(f32)

    def stacked(start, width):
        return jnp.concatenate(
            [
                scratch[:, pl.ds(pl.multiple_of(start, LANES), width)],
                scratch[:, pl.ds(pl.multiple_of(start + width, LANES), width)],
            ],
            axis=0,
        ).astype(bf16)

    message[:, :half] = stacked(narrow_place * (2 * half), half)
    row = lax.broadcasted_iota(jnp.int32, (2 * rows, LANES), 0)
    ids = jnp.zeros((2 * rows, LANES), f32)
    for r in range(rows):
        ids = jnp.where((row == r) | (row == r + rows), index[r].astype(f32), ids)
    message[:, half:] = ids.astype(bf16)
    for k in range(wide):
        target = lax.rem(wide_place + k, wide)
        slices[k][...] = stacked(target * (2 * wide_half), wide_half)


def joined(own, *others):
    rows = own.shape[0] // 2
    values = [block[...].astype(f32) for block in (own, *reversed(others))]
    upper = jnp.concatenate([value[:rows] for value in values], axis=0)
    lower = jnp.concatenate([value[rows:] for value in values], axis=0)
    return upper, lower


def down_kernel(wide, rank3, *refs):
    blocks, down, (sums, ids) = refs[:wide], refs[wide], refs[wide + 1 :]
    wide_place, _ = own_place()
    count = down.shape[0] // rank3
    upper, lower = joined(*blocks)
    half = upper.shape[1] - LANES
    row_ids = upper[:, half:]
    ids[...] = row_ids
    features = jnp.concatenate([upper[:, :half], lower[:, :half]], axis=1).astype(bf16)
    first = wide_place * count
    column_ids = jnp.transpose(row_ids)[:1, :]
    total = jnp.zeros((rank3, features.shape[0]), f32)
    for e in range(count):
        product = lax.dot_general(
            down[e * rank3 : (e + 1) * rank3, :],
            features,
            (((1,), (1,)), ((), ())),
            preferred_element_type=f32,
        )
        total = jnp.where(column_ids == (first + e).astype(f32), product, total)
    rank2, half_rows = 2 * rank3 // 3, features.shape[0] // 2
    sums[: 2 * half_rows, :] = jnp.transpose(total[:rank2])
    sums[2 * half_rows :, :] = jnp.transpose(
        jnp.concatenate([total[rank2:, :half_rows], total[rank2:, half_rows:]], axis=0)
    )


def base_kernel(wide, *refs):
    blocks, sources, out = refs[:wide], refs[wide:-1], refs[-1]
    chunk = 256
    upper, lower = (part.astype(bf16) for part in joined(*blocks))
    half = upper.shape[1]
    offset = 0
    for source in sources:
        for start in range(0, source.shape[1], chunk):
            columns = slice(start, start + chunk)
            out[:, offset + start : offset + start + chunk] = jnp.dot(
                upper, source[:half, columns], preferred_element_type=f32
            ) + jnp.dot(lower, source[half:, columns], preferred_element_type=f32)
        offset += source.shape[1]


LARGEST = 32767.0
STEP_ROWS = 16


def step_of(exponent):
    return jnp.exp2(exponent * 0.25) * (1.0 / LARGEST)


def up_kernel(wide, narrow, base, ids, *refs):
    parts, (query_up, pair_up) = refs[:narrow], refs[narrow : narrow + 2]
    own, *outs = refs[narrow + 2 : narrow + 2 + wide]
    sums, codes = refs[narrow + 2 + wide :]
    wide_place, _ = own_place()
    count, _, rank, pair_width = pair_up.shape
    all_rows, width = base.shape
    rows = all_rows // wide
    total = parts[0][...]
    for part in parts[1:]:
        total = total + part[...]
    rank_sums = total.astype(bf16).astype(f32)
    last = rank_sums[all_rows:]
    pieces = (
        rank_sums[:all_rows, :rank],
        rank_sums[:all_rows, rank:],
        jnp.concatenate([last[:, :rank], last[:, rank:]], axis=0),
    )
    row_ids = ids[:, :1]
    first = wide_place * count

    def widen(p):
        return jnp.concatenate(
            [jnp.where(row_ids == (first + e).astype(f32), pieces[p], 0.0) for e in range(count)],
            axis=1,
        ).astype(bf16)

    chunk = 256
    query_width = query_up.shape[1]
    pairs = [
        jnp.concatenate([pair_up[e, p] for e in range(count)], axis=0) for p in range(2)
    ]
    groups = (
        (widen(0), query_up, 0, query_width),
        (widen(1), pairs[0], query_width, pair_width),
        (widen(2), pairs[1], query_width + pair_width, pair_width),
    )
    exponents = []
    for lhs, weights, offset, group_width in groups:
        top = jnp.zeros((all_rows, LANES), f32)
        for start in range(0, group_width, chunk):
            columns = slice(offset + start, offset + start + chunk)
            values = base[:, columns] + adapter_scale * jnp.dot(
                lhs, weights[:, start : start + chunk], preferred_element_type=f32
            )
            sums[:, columns] = values
            for j in range(0, chunk, LANES):
                top = jnp.maximum(top, jnp.abs(values[:, j : j + LANES]))
        top = jnp.maximum(jnp.max(top, axis=-1, keepdims=True), 1e-30)
        exponents.append(jnp.ceil(4.0 * jnp.log2(top) + 0.01))
    for (_, _, offset, group_width), exponent in zip(groups, exponents):
        inverse = 1.0 / step_of(exponent)
        for start in range(offset, offset + group_width, LANES):
            values = sums[:, start : start + LANES]
            window = slice(start // LANES * rows, (start // LANES + 1) * rows)
            own[window, :] = values[:rows]
            rounded = jnp.round(values * inverse)
            for k in range(1, wide):
                codes[k - 1, window, :] = rounded[k * rows : (k + 1) * rows]
    lane = lax.broadcasted_iota(jnp.int32, (all_rows, LANES), 1)
    marks = jnp.where(
        lane < 32, exponents[0], jnp.where(lane < 64, exponents[1], exponents[2])
    )
    body = width // LANES * rows
    rest = jnp.zeros((outs[0].shape[0] - body - rows, LANES), f32)
    for k in range(1, wide):
        mark = jnp.concatenate([marks[k * rows : (k + 1) * rows], rest], axis=0)
        outs[k - 1][:body, :] = codes[k - 1].astype(jnp.int32).astype(jnp.int16)
        outs[k - 1][body:, :] = mark.astype(jnp.int32).astype(jnp.int16)


def attend_kernel(wide, heads, kv_heads, visible, cosine, sine, *refs):
    parts, (keys, values, out, rotated, attended) = refs[:wide], refs[wide:]
    rows, _, _, width = keys.shape
    group = heads // kv_heads
    body = (heads + 2 * kv_heads) * rows
    total = parts[0][...]
    for part in parts[1:]:
        steps = step_of(part[body:, :].astype(jnp.int32).astype(f32)[:rows])
        query_step, key_step, value_step = (
            jnp.broadcast_to(steps[:, lane : lane + 1], (rows, width)) for lane in (0, 32, 64)
        )
        step = jnp.concatenate(
            [query_step] * heads + [key_step] * kv_heads + [value_step] * kv_heads, axis=0
        )
        total = total + part[:body, :].astype(jnp.int32).astype(f32) * step
    turned = (heads + kv_heads) * rows
    straight = total[:turned]
    straight = straight * cosine[...] + pltpu.roll(straight, width // 2, 1) * sine[...]
    rotated[:turned] = straight.astype(bf16).astype(f32)
    rotated[turned:] = total[turned:].astype(bf16).astype(f32)
    factor = 1.0 / math.sqrt(width)
    pairs = [(r, g) for r in range(rows) for g in range(kv_heads)]
    scores, own = [], []
    for r, g in pairs:
        query = rotated[pl.ds(g * group * rows + r, group, stride=rows), :]
        new_key = rotated[pl.ds((heads + g) * rows + r, 1), :]
        score = lax.dot_general(
            query.astype(bf16), keys[r, g], (((1,), (1,)), ((), ())), preferred_element_type=f32
        )
        scores.append(score * factor + visible[r : r + 1, :])
        own.append(jnp.sum(query * new_key, axis=-1, keepdims=True) * factor)
    score, own = jnp.concatenate(scores, axis=0), jnp.concatenate(own, axis=0)
    row_max = jnp.maximum(jnp.max(score, axis=-1, keepdims=True), own)
    weights = jnp.exp(score - row_max)
    own_weight = jnp.exp(own - row_max)
    denominator = jnp.sum(weights, axis=-1, keepdims=True) + own_weight
    share = 1.0 / denominator
    weights = (weights * share).astype(bf16)
    own_weight = (own_weight * share).astype(bf16).astype(f32)
    mixed = []
    for i, (r, g) in enumerate(pairs):
        new_value = rotated[pl.ds((heads + kv_heads + g) * rows + r, 1), :]
        window = slice(i * group, (i + 1) * group)
        mixed.append(
            jnp.dot(weights[window], values[r, g], preferred_element_type=f32)
            + own_weight[window] * new_value
        )
    for i, (r, g) in enumerate(pairs):
        attended[pl.ds(g * group * rows + r, group, stride=rows), :] = mixed[i]
    for h in range(heads):
        out[:, h * width : (h + 1) * width] = attended[h * rows : (h + 1) * rows, :].astype(bf16)


def rotation_kernel(lengths_far, after, cosine, sine, visible, lengths, sem):
    copy = pltpu.make_async_copy(lengths_far, lengths, sem)
    copy.start()
    rows, positions = visible.shape
    half_dim = HEAD_WIDTH // 2
    lane = lax.broadcasted_iota(jnp.int32, (rows, HEAD_WIDTH), 1)
    place = jnp.where(lane < half_dim, lane, lane - half_dim).astype(f32)
    frequency = jnp.exp(place * (-2.0 / HEAD_WIDTH * math.log(rope_base)))
    row = lax.broadcasted_iota(jnp.int32, (rows, positions), 0)
    length = jnp.zeros((rows, positions), jnp.int32)
    copy.wait()
    for r in range(rows):
        length = jnp.where(row == r, lengths[r], length)
    position = lax.broadcasted_iota(jnp.int32, (rows, positions), 1)
    visible[...] = jnp.where(position < length, 0.0, -jnp.inf)
    angles = length[:, :HEAD_WIDTH].astype(f32) * frequency
    cosines = jnp.cos(angles)
    sines = jnp.where(lane < half_dim, -1.0, 1.0) * jnp.sin(angles)
    repeats = cosine.shape[0] // rows
    cosine[...] = jnp.concatenate([cosines] * repeats, axis=0)
    sine[...] = jnp.concatenate([sines] * repeats, axis=0)


def shifted(count, k):
    return [(i, (i + k) % count) for i in range(count)]


def on_device(
    hidden,
    attention_norm_gain,
    row_adapter_index,
    lengths,
    paged_key_cache,
    paged_value_cache,
    query_weight,
    key_weight,
    value_weight,
    adapter_down_weight,
    adapter_up_query,
    adapter_up_key_value,
):
    wide, narrow = lax.axis_size("wide"), lax.axis_size("narrow")
    rows, features = hidden.shape
    count, _, rank, slice_width = adapter_down_weight.shape
    query_width, kv_width = query_weight.shape[1], key_weight.shape[1]
    heads, kv_heads = query_width // HEAD_WIDTH, kv_width // HEAD_WIDTH
    all_rows = rows * wide
    rank3 = 3 * rank
    width = query_width + 2 * kv_width
    half, wide_half = slice_width // 2, query_weight.shape[0] // 2

    message, *slices = call(
        functools.partial(normalize_kernel, wide),
        [shape_of((2 * rows, half + LANES), bf16)] + [shape_of((2 * rows, wide_half), bf16)] * wide,
        [HBM, HBM, HBM],
        [
            pltpu.with_memory_space_constraint(x, pltpu.HBM)
            for x in (row_adapter_index, hidden, attention_norm_gain)
        ],
        [
            pltpu.VMEM((rows, features), f32),
            pltpu.SMEM((rows,), jnp.int32),
            pltpu.VMEM((rows, features), bf16),
            pltpu.VMEM((features,), bf16),
            pltpu.SemaphoreType.DMA((3,)),
        ],
        flops=10**10,
    )
    blocks = [
        lax.ppermute(message, "wide", shifted(wide, k)) for k in range(wide - 1, 0, -1)
    ]
    wide_blocks = [
        lax.ppermute(slices[k], "wide", shifted(wide, k)) for k in range(wide - 1, 0, -1)
    ]
    down = adapter_down_weight.reshape(count * rank3, slice_width)
    sums, ids = call(
        functools.partial(down_kernel, wide, rank3),
        [shape_of((all_rows * 3 // 2, 2 * rank), f32), shape_of((all_rows, LANES), f32)],
        [VMEM] * wide + [VMEM],
        (message, *blocks, down),
        vmem=12,
        flops=2 * all_rows * down.size,
        nbytes=2 * down.size,
    )
    parts = [sums] + [lax.ppermute(sums, "narrow", shifted(narrow, k)) for k in range(1, narrow)]
    weights = (query_weight, key_weight, value_weight)
    base = call(
        functools.partial(base_kernel, wide),
        shape_of((all_rows, width), f32),
        [VMEM] * wide + [VMEM] * 3,
        (slices[0], *wide_blocks, *weights),
        vmem=16,
        flops=4 * all_rows * width * wide_half,
        nbytes=4 * width * wide_half,
    )
    query_up = adapter_up_query.reshape(count * rank, query_width)
    body = width // LANES * rows
    step_rows = -(-rows // STEP_ROWS) * STEP_ROWS
    outs = call(
        functools.partial(up_kernel, wide, narrow),
        [shape_of((body, LANES), f32)]
        + [shape_of((body + step_rows, LANES), jnp.int16)] * (wide - 1),
        [VMEM, VMEM] + [VMEM] * narrow + [VMEM] * 2,
        (base, ids, *parts, query_up, adapter_up_key_value),
        [pltpu.VMEM((all_rows, width), f32), pltpu.VMEM((wide - 1, body, LANES), f32)],
        vmem=10 + wide // 2,
        flops=2 * all_rows * width * count * rank,
        nbytes=2 * width * count * rank,
    )
    gathered = [outs[0]] + [
        lax.ppermute(outs[k], "wide", shifted(wide, -k))
        for k in (LAST_ORDER if wide == 4 else range(1, wide))
    ]
    turned = (heads + kv_heads) * rows
    cosine, sine, visible = call(
        rotation_kernel,
        [shape_of((turned, LANES), f32)] * 2 + [shape_of((rows, paged_key_cache.shape[2]), f32)],
        [HBM, ANY],
        (pltpu.with_memory_space_constraint(lengths, pltpu.HBM), outs[0]),
        [pltpu.SMEM((rows,), jnp.int32), pltpu.SemaphoreType.DMA],
    )
    return call(
        functools.partial(attend_kernel, wide, heads, kv_heads),
        shape_of((rows, query_width), bf16),
        [VMEM] * (3 + wide + 2),
        (visible, cosine, sine, *gathered, paged_key_cache, paged_value_cache),
        [
            pltpu.VMEM((body, LANES), f32),
            pltpu.VMEM((heads * rows + 2 * STEP_ROWS, LANES), f32),
        ],
        vmem=8 + wide // 4,
        flops=4 * paged_key_cache.size * 8,
        nbytes=4 * paged_key_cache.size,
    )


def solution(mesh):
    in_specs = (
        P(("groups", "wide"), None),
        P(),
        P(("groups", "wide")),
        P(("groups", "wide")),
        P(("groups", "wide"), "narrow", None, None),
        P(("groups", "wide"), "narrow", None, None),
        P("wide", "narrow"),
        P("wide", "narrow"),
        P("wide", "narrow"),
        P(("groups", "wide"), None, None, "narrow"),
        P(("groups", "wide"), None, "narrow"),
        P(("groups", "wide"), None, None, "narrow"),
    )
    out_specs = P(("groups", "wide"), "narrow")
    return jax.shard_map(
        on_device, mesh=mesh, in_specs=in_specs, out_specs=out_specs, check_vma=False
    )
```

```python
import functools
import math

import jax
import jax.numpy as jnp
from jax import lax
from jax.experimental import pallas as pl
from jax.experimental.pallas import tpu as pltpu
from jax.sharding import PartitionSpec as P

HEAD_WIDTH = 128
LANES = 128

adapter_scale = 0.5
rope_base = 500000.0
epsilon = 1e-05

LAST_ORDER = (2, 3, 1)

f32 = jnp.float32
bf16 = jnp.bfloat16

VMEM = pl.BlockSpec(memory_space=pltpu.VMEM)
ANY = pl.BlockSpec(memory_space=pl.ANY)
HBM = pl.BlockSpec(memory_space=pltpu.HBM)


def shape_of(shape, dtype):
    return jax.ShapeDtypeStruct(shape, dtype)


def call(kernel, outs, in_specs, args, scratch=(), flops=0, nbytes=0, vmem=8):
    return pl.pallas_call(
        kernel,
        out_shape=outs,
        in_specs=in_specs,
        out_specs=jax.tree.map(lambda _: VMEM, outs),
        scratch_shapes=scratch,
        compiler_params=pltpu.CompilerParams(vmem_limit_bytes=vmem * 2**20),
        cost_estimate=pl.CostEstimate(flops=flops, bytes_accessed=nbytes, transcendentals=0),
    )(*args)


def own_place():
    return lax.axis_index("wide"), lax.axis_index("narrow")


def normalize_kernel(wide, index_far, hidden_far, gain_far, message, *refs):
    slices, (scratch, index, hidden, gain, sems) = refs[:wide], refs[wide:]
    copies = [
        pltpu.make_async_copy(far, near, sems.at[i])
        for i, (far, near) in enumerate(
            ((hidden_far, hidden), (gain_far, gain), (index_far, index))
        )
    ]
    for copy in copies:
        copy.start()
    wide_place, narrow_place = own_place()
    rows = hidden.shape[0]
    half = message.shape[1] - LANES
    wide_half = slices[0].shape[1]
    copies[0].wait()
    values = hidden[...].astype(f32)
    factor = lax.rsqrt(jnp.mean(values * values, axis=-1, keepdims=True) + epsilon)
    copies[1].wait()
    copies[2].wait()
    scale = gain[...].astype(f32).reshape(1, -1)
    normed = (values * factor * scale).astype(bf16)
    scratch[...] = normed.astype(f32)

    def stacked(start, width):
        return jnp.concatenate(
            [
                scratch[:, pl.ds(pl.multiple_of(start, LANES), width)],
                scratch[:, pl.ds(pl.multiple_of(start + width, LANES), width)],
            ],
            axis=0,
        ).astype(bf16)

    message[:, :half] = stacked(narrow_place * (2 * half), half)
    row = lax.broadcasted_iota(jnp.int32, (2 * rows, LANES), 0)
    ids = jnp.zeros((2 * rows, LANES), f32)
    for r in range(rows):
        ids = jnp.where((row == r) | (row == r + rows), index[r].astype(f32), ids)
    message[:, half:] = ids.astype(bf16)
    for k in range(wide):
        target = lax.rem(wide_place + k, wide)
        slices[k][...] = stacked(target * (2 * wide_half), wide_half)


def joined(own, *others):
    rows = own.shape[0] // 2
    values = [block[...].astype(f32) for block in (own, *reversed(others))]
    upper = jnp.concatenate([value[:rows] for value in values], axis=0)
    lower = jnp.concatenate([value[rows:] for value in values], axis=0)
    return upper, lower


def down_kernel(wide, rank3, *refs):
    blocks, down, (sums, ids) = refs[:wide], refs[wide], refs[wide + 1 :]
    wide_place, _ = own_place()
    count = down.shape[0] // rank3
    upper, lower = joined(*blocks)
    half = upper.shape[1] - LANES
    row_ids = upper[:, half:]
    ids[...] = row_ids
    features = jnp.concatenate([upper[:, :half], lower[:, :half]], axis=1).astype(bf16)
    first = wide_place * count
    column_ids = jnp.transpose(row_ids)[:1, :]
    total = jnp.zeros((rank3, features.shape[0]), f32)
    for e in range(count):
        product = lax.dot_general(
            down[e * rank3 : (e + 1) * rank3, :],
            features,
            (((1,), (1,)), ((), ())),
            preferred_element_type=f32,
        )
        total = jnp.where(column_ids == (first + e).astype(f32), product, total)
    rank2, half_rows = 2 * rank3 // 3, features.shape[0] // 2
    sums[: 2 * half_rows, :] = jnp.transpose(total[:rank2])
    sums[2 * half_rows :, :] = jnp.transpose(
        jnp.concatenate([total[rank2:, :half_rows], total[rank2:, half_rows:]], axis=0)
    )


def base_kernel(wide, *refs):
    blocks, sources, out = refs[:wide], refs[wide:-1], refs[-1]
    chunk = 256
    upper, lower = (part.astype(bf16) for part in joined(*blocks))
    features = jnp.concatenate([upper, lower], axis=1)
    offset = 0
    for source in sources:
        for start in range(0, source.shape[1], chunk):
            columns = slice(start, start + chunk)
            out[:, offset + start : offset + start + chunk] = jnp.dot(
                features, source[:, columns], preferred_element_type=f32
            )
        offset += source.shape[1]


LARGEST = 32767.0
STEP_ROWS = 16


def step_of(exponent):
    return jnp.exp2(exponent * 0.25) * (1.0 / LARGEST)


def up_kernel(wide, narrow, base, ids, *refs):
    parts, (query_up, pair_up) = refs[:narrow], refs[narrow : narrow + 2]
    own, *outs = refs[narrow + 2 : narrow + 2 + wide]
    sums, codes = refs[narrow + 2 + wide :]
    wide_place, _ = own_place()
    count, _, rank, pair_width = pair_up.shape
    all_rows, width = base.shape
    rows = all_rows // wide
    total = parts[0][...]
    for part in parts[1:]:
        total = total + part[...]
    rank_sums = total.astype(bf16).astype(f32)
    last = rank_sums[all_rows:]
    pieces = (
        rank_sums[:all_rows, :rank],
        rank_sums[:all_rows, rank:],
        jnp.concatenate([last[:, :rank], last[:, rank:]], axis=0),
    )
    row_ids = ids[:, :1]
    first = wide_place * count

    def widen(p):
        return jnp.concatenate(
            [jnp.where(row_ids == (first + e).astype(f32), pieces[p], 0.0) for e in range(count)],
            axis=1,
        ).astype(bf16)

    chunk = 256
    query_width = query_up.shape[1]
    pairs = [
        jnp.concatenate([pair_up[e, p] for e in range(count)], axis=0) for p in range(2)
    ]
    groups = (
        (widen(0), query_up, 0, query_width),
        (widen(1), pairs[0], query_width, pair_width),
        (widen(2), pairs[1], query_width + pair_width, pair_width),
    )
    exponents = []
    for lhs, weights, offset, group_width in groups:
        top = jnp.zeros((all_rows, LANES), f32)
        for start in range(0, group_width, chunk):
            columns = slice(offset + start, offset + start + chunk)
            values = base[:, columns] + adapter_scale * jnp.dot(
                lhs, weights[:, start : start + chunk], preferred_element_type=f32
            )
            sums[:, columns] = values
            for j in range(0, chunk, LANES):
                top = jnp.maximum(top, jnp.abs(values[:, j : j + LANES]))
        top = jnp.maximum(jnp.max(top, axis=-1, keepdims=True), 1e-30)
        exponents.append(jnp.ceil(4.0 * jnp.log2(top) + 0.01))
    for (_, _, offset, group_width), exponent in zip(groups, exponents):
        inverse = 1.0 / step_of(exponent)
        for start in range(offset, offset + group_width, LANES):
            values = sums[:, start : start + LANES]
            window = slice(start // LANES * rows, (start // LANES + 1) * rows)
            own[window, :] = values[:rows]
            rounded = jnp.round(values * inverse)
            for k in range(1, wide):
                codes[k - 1, window, :] = rounded[k * rows : (k + 1) * rows]
    lane = lax.broadcasted_iota(jnp.int32, (all_rows, LANES), 1)
    marks = jnp.where(
        lane < 32, exponents[0], jnp.where(lane < 64, exponents[1], exponents[2])
    )
    body = width // LANES * rows
    rest = jnp.zeros((outs[0].shape[0] - body - rows, LANES), f32)
    for k in range(1, wide):
        mark = jnp.concatenate([marks[k * rows : (k + 1) * rows], rest], axis=0)
        outs[k - 1][:body, :] = codes[k - 1].astype(jnp.int32).astype(jnp.int16)
        outs[k - 1][body:, :] = mark.astype(jnp.int32).astype(jnp.int16)


def attend_kernel(wide, heads, kv_heads, visible, cosine, sine, *refs):
    parts, (keys, values, out, rotated, attended) = refs[:wide], refs[wide:]
    rows, _, width, _ = keys.shape
    group = heads // kv_heads
    body = (heads + 2 * kv_heads) * rows
    total = parts[0][...]
    for part in parts[1:]:
        steps = step_of(part[body:, :].astype(jnp.int32).astype(f32)[:rows])
        query_step, key_step, value_step = (
            jnp.broadcast_to(steps[:, lane : lane + 1], (rows, width)) for lane in (0, 32, 64)
        )
        step = jnp.concatenate(
            [query_step] * heads + [key_step] * kv_heads + [value_step] * kv_heads, axis=0
        )
        total = total + part[:body, :].astype(jnp.int32).astype(f32) * step
    turned = (heads + kv_heads) * rows
    straight = total[:turned]
    straight = straight * cosine[...] + pltpu.roll(straight, width // 2, 1) * sine[...]
    rotated[:turned] = straight.astype(bf16).astype(f32)
    rotated[turned:] = total[turned:].astype(bf16).astype(f32)
    factor = 1.0 / math.sqrt(width)
    pairs = [(r, g) for r in range(rows) for g in range(kv_heads)]
    nothing = jnp.zeros((group, width), bf16)
    scores, own = [], []
    for r in range(rows):
        spread = []
        for g in range(kv_heads):
            query = rotated[pl.ds(g * group * rows + r, group, stride=rows), :]
            new_key = rotated[pl.ds((heads + g) * rows + r, 1), :]
            own.append(jnp.sum(query * new_key, axis=-1, keepdims=True) * factor)
            spread.append(
                jnp.concatenate(
                    [query.astype(bf16) if i == g else nothing for i in range(kv_heads)], axis=1
                )
            )
        score = jnp.dot(
            jnp.concatenate(spread, axis=0),
            keys[r].reshape(kv_heads * width, keys.shape[3]),
            preferred_element_type=f32,
        )
        scores.append(score * factor + visible[r : r + 1, :])
    score, own = jnp.concatenate(scores, axis=0), jnp.concatenate(own, axis=0)
    row_max = jnp.maximum(jnp.max(score, axis=-1, keepdims=True), own)
    weights = jnp.exp(score - row_max)
    own_weight = jnp.exp(own - row_max)
    denominator = jnp.sum(weights, axis=-1, keepdims=True) + own_weight
    share = 1.0 / denominator
    weights = (weights * share).astype(bf16)
    own_weight = (own_weight * share).astype(bf16).astype(f32)
    mixed = []
    for r in range(rows):
        window = slice(r * kv_heads * group, (r + 1) * kv_heads * group)
        both = jnp.dot(
            weights[window],
            jnp.concatenate([values[r, g] for g in range(kv_heads)], axis=1),
            preferred_element_type=f32,
        )
        for g in range(kv_heads):
            new_value = rotated[pl.ds((heads + kv_heads + g) * rows + r, 1), :]
            place = slice(g * group, (g + 1) * group)
            mixed.append(
                both[place, g * width : (g + 1) * width] + own_weight[window][place] * new_value
            )
    for i, (r, g) in enumerate(pairs):
        attended[pl.ds(g * group * rows + r, group, stride=rows), :] = mixed[i]
    for h in range(heads):
        out[:, h * width : (h + 1) * width] = attended[h * rows : (h + 1) * rows, :].astype(bf16)


def ready_kernel(lengths_far, after, keys, cosine, sine, visible, turned_keys, lengths, sem):
    copy = pltpu.make_async_copy(lengths_far, lengths, sem)
    copy.start()
    rows, positions = visible.shape
    half_dim = HEAD_WIDTH // 2
    lane = lax.broadcasted_iota(jnp.int32, (rows, HEAD_WIDTH), 1)
    place = jnp.where(lane < half_dim, lane, lane - half_dim).astype(f32)
    frequency = jnp.exp(place * (-2.0 / HEAD_WIDTH * math.log(rope_base)))
    row = lax.broadcasted_iota(jnp.int32, (rows, positions), 0)
    length = jnp.zeros((rows, positions), jnp.int32)
    copy.wait()
    for r in range(rows):
        length = jnp.where(row == r, lengths[r], length)
    position = lax.broadcasted_iota(jnp.int32, (rows, positions), 1)
    visible[...] = jnp.where(position < length, 0.0, -jnp.inf)
    angles = length[:, :HEAD_WIDTH].astype(f32) * frequency
    cosines = jnp.cos(angles)
    sines = jnp.where(lane < half_dim, -1.0, 1.0) * jnp.sin(angles)
    repeats = cosine.shape[0] // rows
    cosine[...] = jnp.concatenate([cosines] * repeats, axis=0)
    sine[...] = jnp.concatenate([sines] * repeats, axis=0)
    for r in range(rows):
        for g in range(keys.shape[1]):
            turned_keys[r, g] = jnp.transpose(keys[r, g])


def shifted(count, k):
    return [(i, (i + k) % count) for i in range(count)]


def on_device(
    hidden,
    attention_norm_gain,
    row_adapter_index,
    lengths,
    paged_key_cache,
    paged_value_cache,
    query_weight,
    key_weight,
    value_weight,
    adapter_down_weight,
    adapter_up_query,
    adapter_up_key_value,
):
    wide, narrow = lax.axis_size("wide"), lax.axis_size("narrow")
    rows, features = hidden.shape
    count, _, rank, slice_width = adapter_down_weight.shape
    query_width, kv_width = query_weight.shape[1], key_weight.shape[1]
    heads, kv_heads = query_width // HEAD_WIDTH, kv_width // HEAD_WIDTH
    all_rows = rows * wide
    rank3 = 3 * rank
    width = query_width + 2 * kv_width
    half, wide_half = slice_width // 2, query_weight.shape[0] // 2

    message, *slices = call(
        functools.partial(normalize_kernel, wide),
        [shape_of((2 * rows, half + LANES), bf16)] + [shape_of((2 * rows, wide_half), bf16)] * wide,
        [HBM, HBM, HBM],
        [
            pltpu.with_memory_space_constraint(x, pltpu.HBM)
            for x in (row_adapter_index, hidden, attention_norm_gain)
        ],
        [
            pltpu.VMEM((rows, features), f32),
            pltpu.SMEM((rows,), jnp.int32),
            pltpu.VMEM((rows, features), bf16),
            pltpu.VMEM((features,), bf16),
            pltpu.SemaphoreType.DMA((3,)),
        ],
        flops=10**10,
    )
    blocks = [
        lax.ppermute(message, "wide", shifted(wide, k)) for k in range(wide - 1, 0, -1)
    ]
    wide_blocks = [
        lax.ppermute(slices[k], "wide", shifted(wide, k)) for k in range(wide - 1, 0, -1)
    ]
    down = adapter_down_weight.reshape(count * rank3, slice_width)
    sums, ids = call(
        functools.partial(down_kernel, wide, rank3),
        [shape_of((all_rows * 3 // 2, 2 * rank), f32), shape_of((all_rows, LANES), f32)],
        [VMEM] * wide + [VMEM],
        (message, *blocks, down),
        vmem=12,
        flops=2 * all_rows * down.size,
        nbytes=2 * down.size,
    )
    parts = [sums] + [lax.ppermute(sums, "narrow", shifted(narrow, k)) for k in range(1, narrow)]
    weights = (query_weight, key_weight, value_weight)
    base = call(
        functools.partial(base_kernel, wide),
        shape_of((all_rows, width), f32),
        [VMEM] * wide + [VMEM] * 3,
        (slices[0], *wide_blocks, *weights),
        vmem=16,
        flops=4 * all_rows * width * wide_half,
        nbytes=4 * width * wide_half,
    )
    query_up = adapter_up_query.reshape(count * rank, query_width)
    body = width // LANES * rows
    step_rows = -(-rows // STEP_ROWS) * STEP_ROWS
    outs = call(
        functools.partial(up_kernel, wide, narrow),
        [shape_of((body, LANES), f32)]
        + [shape_of((body + step_rows, LANES), jnp.int16)] * (wide - 1),
        [VMEM, VMEM] + [VMEM] * narrow + [VMEM] * 2,
        (base, ids, *parts, query_up, adapter_up_key_value),
        [pltpu.VMEM((all_rows, width), f32), pltpu.VMEM((wide - 1, body, LANES), f32)],
        vmem=10 + wide // 2,
        flops=2 * all_rows * width * count * rank,
        nbytes=2 * width * count * rank,
    )
    gathered = [outs[0]] + [
        lax.ppermute(outs[k], "wide", shifted(wide, -k))
        for k in (LAST_ORDER if wide == 4 else range(1, wide))
    ]
    turned = (heads + kv_heads) * rows
    positions = paged_key_cache.shape[2]
    cosine, sine, visible, turned_keys = call(
        ready_kernel,
        [shape_of((turned, LANES), f32)] * 2
        + [shape_of((rows, positions), f32)]
        + [shape_of((rows, kv_heads, HEAD_WIDTH, positions), bf16)],
        [HBM, ANY, VMEM],
        (pltpu.with_memory_space_constraint(lengths, pltpu.HBM), outs[0], paged_key_cache),
        [pltpu.SMEM((rows,), jnp.int32), pltpu.SemaphoreType.DMA],
    )
    return call(
        functools.partial(attend_kernel, wide, heads, kv_heads),
        shape_of((rows, query_width), bf16),
        [VMEM] * (3 + wide + 2),
        (visible, cosine, sine, *gathered, turned_keys, paged_value_cache),
        [
            pltpu.VMEM((body, LANES), f32),
            pltpu.VMEM((heads * rows + 2 * STEP_ROWS, LANES), f32),
        ],
        vmem=8 + wide // 4,
        flops=4 * paged_key_cache.size * 8,
        nbytes=4 * paged_key_cache.size,
    )


def solution(mesh):
    in_specs = (
        P(("groups", "wide"), None),
        P(),
        P(("groups", "wide")),
        P(("groups", "wide")),
        P(("groups", "wide"), "narrow", None, None),
        P(("groups", "wide"), "narrow", None, None),
        P("wide", "narrow"),
        P("wide", "narrow"),
        P("wide", "narrow"),
        P(("groups", "wide"), None, None, "narrow"),
        P(("groups", "wide"), None, "narrow"),
        P(("groups", "wide"), None, None, "narrow"),
    )
    out_specs = P(("groups", "wide"), "narrow")
    return jax.shard_map(
        on_device, mesh=mesh, in_specs=in_specs, out_specs=out_specs, check_vma=False
    )
```
